256 devices in a mesh: rep: 64 (over x, y, z_hi, core), fsdp: 4 (over z_lo).
Axes of the slice: x: 4, y: 4, z: 8 (z_hi: 2, z_lo: 4; z = z_hi * 4 + z_lo), core: 2. Of those that a mesh axis runs over, the one named last changes fastest.
Arguments:
- activations: bfloat16 [65536, 8192], P(('rep', 'fsdp')), may hold values from -6 to 6
- norm_gain: bfloat16 [64, 8192], P('rep', 'fsdp'), may hold values from 0.5 to 1.5
- key_weight: bfloat16 [64, 8192, 512], P('rep', 'fsdp'), may hold values from -6 to 6
- key_cotangent: bfloat16 [65536, 512], P(('rep', 'fsdp')), may hold values from -6 to 6
- outer_params: float32 [8192, 128], P('fsdp'), may hold values from -6 to 6
- outer_momentum: float32 [8192, 128], P('fsdp'), may hold values from -3 to 3
- fragment: int32 [1], replicated, may hold values from 0 to 1048575
Outputs:
- keys: bfloat16 [65536, 512], P(('rep', 'fsdp'))
- input_grad: bfloat16 [65536, 8192], P(('rep', 'fsdp'))
- weight_grad: bfloat16 [64, 8192, 512], P('rep', 'fsdp')
- gain_grad: float32 [64, 8192], P('rep', 'fsdp')
- new_params: float32 [8192, 128], P('fsdp')
- new_momentum: float32 [8192, 128], P('fsdp')
The draws below stay inside these ranges and needn't reach their ends.
All inputs are finite; a program needn't handle non-finite values.
Results may differ from the reference program's by a relative error of at most 0.015.
Values may be sent and summed in bfloat16 or wider, within the bound.
No kernel may reach another device: no remote copies, remote signals or barrier semaphores. Data moves between devices by JAX's collectives and lax.ppermute only.
A program may use at most 128 MiB of HBM per device.

```python
import jax
import jax.numpy as jnp
from jax import lax

D = 8192
HEAD = 128
HEADS = 4
TOK_DEV = 256
KEY_WIDTH = 512
REPLICAS = 64
TOKENS = 65536
N_REP = 64
N_FSDP = 4


def levels(key, shape, pieces, low, largest):
    def one(axis_at, blocks):
        steps = jax.random.uniform(jax.random.fold_in(jax.random.fold_in(key, 6), axis_at), (blocks,), jnp.float32, low / len(pieces), largest / len(pieces))
        return jnp.repeat(jnp.exp(steps), shape[axis_at] // blocks).reshape((-1,) + (1,) * (len(shape) - axis_at - 1))

    gain = one(*pieces[0])
    for cut in pieces[1:]:
        gain = gain * one(*cut)
    return gain


def scatter_about(rng, dims, scale, reach, split=(), kind=jnp.bfloat16):
    entries = scale * jax.random.normal(rng, dims, jnp.float32)
    if split:
        entries = entries * levels(rng, dims, split, -0.22, 0.18)
    return jnp.clip(entries, -reach, reach).astype(kind)


def setup_inputs(seed: int = 0) -> dict:
    streams_of = jax.random.split(jax.random.key(seed), 8)
    return {
        "activations": scatter_about(streams_of[0], (TOKENS, D), 1.0, 6.0, ((0, 256),)),
        "norm_gain": jnp.clip(1.0 + 0.1 * jax.random.normal(streams_of[1], (REPLICAS, D), jnp.float32), 0.5, 1.5).astype(jnp.bfloat16),
        "key_weight": scatter_about(streams_of[2], (REPLICAS, D, KEY_WIDTH), 1.0, 6.0, ((0, 64), (1, 4))),
        "key_cotangent": scatter_about(streams_of[3], (TOKENS, KEY_WIDTH), 1.0, 6.0, ((0, 256),)),
        "outer_params": scatter_about(streams_of[4], (D, HEAD), 1.0, 6.0, ((0, 4),), jnp.float32),
        "outer_momentum": scatter_about(streams_of[5], (D, HEAD), 0.5, 3.0, ((0, 4),), jnp.float32),
        "fragment": jax.random.randint(streams_of[6], (1,), 0, 1048576).astype(jnp.int32),
    }


outer_rate = 0.7
momentum_decay = 0.9
epsilon = 1e-05

def replica_window(inputs):
    activation_rows, gain_row, weight_matrix, cotangent_rows = inputs
    factor = D ** (-0.5)
    xfloat = activation_rows.astype(jnp.float32)
    inverse = lax.rsqrt(lax.optimization_barrier(jnp.mean(xfloat * xfloat, axis=1, keepdims=True)) + epsilon)
    normed = xfloat * inverse
    gain_full = gain_row.astype(jnp.float32)
    hidden = (normed * gain_full).astype(jnp.bfloat16)
    keys = (jnp.dot(hidden, weight_matrix, preferred_element_type=jnp.float32) * factor).astype(jnp.bfloat16)
    upstream = jnp.dot(cotangent_rows, weight_matrix.T, preferred_element_type=jnp.float32) * factor
    adjusted = upstream * gain_full
    project = lax.optimization_barrier(jnp.mean(adjusted * normed, axis=1, keepdims=True))
    input_grad = (inverse * (adjusted - normed * project)).astype(jnp.bfloat16)
    gain_grad = lax.optimization_barrier(jnp.sum(upstream * normed, axis=0))
    hidden_blocks = hidden.reshape(N_FSDP, TOK_DEV, D).astype(jnp.float32)
    cotangent_blocks = cotangent_rows.reshape(N_FSDP, TOK_DEV, KEY_WIDTH).astype(jnp.float32)
    partials = jnp.einsum('str,stk->srk', hidden_blocks, cotangent_blocks) * factor
    partials = partials.astype(jnp.bfloat16)
    weight_grad = lax.optimization_barrier(jnp.sum(partials.astype(jnp.float32), axis=0)).astype(jnp.bfloat16)
    return (keys, input_grad, weight_grad, gain_grad)

def reference(activations, norm_gain, key_weight, key_cotangent, outer_params, outer_momentum, fragment):
    rows_replica = N_FSDP * TOK_DEV
    keys, input_grad, weight_grad, gain_grad = lax.map(replica_window, (activations.reshape(N_REP, rows_replica, D), norm_gain, key_weight, key_cotangent.reshape(N_REP, rows_replica, KEY_WIDTH)))
    column_start = (fragment[0] % HEADS * HEAD).astype(jnp.int32)
    local_block = lax.dynamic_slice_in_dim(key_weight, column_start, HEAD, 2).astype(jnp.float32)
    summed_delta = lax.optimization_barrier(jnp.sum(outer_params[None] - local_block, axis=0))
    increment = summed_delta / N_REP
    new_momentum = momentum_decay * outer_momentum + increment
    new_params = outer_params - outer_rate * (increment + momentum_decay * new_momentum)
    return (keys.reshape(TOKENS, KEY_WIDTH), input_grad.reshape(TOKENS, D), weight_grad, gain_grad, new_params, new_momentum)
```

```python
import jax
import jax.numpy as jnp
from jax import lax
from jax.sharding import Mesh, PartitionSpec as P

outer_rate = 0.7
momentum_decay = 0.9
epsilon = 1e-05

PIECES = 2
RIGHT = [(0, 1), (1, 2), (2, 3)]
LEFT = [(1, 0), (2, 1), (3, 2)]
CONTRACT_ROWS = (((0,), (0,)), ((), ()))
CONTRACT_COLUMNS = (((1,), (1,)), ((), ()))
f32, bf16 = jnp.float32, jnp.bfloat16


def dot(a, b, dims=(((1,), (0,)), ((), ()))):
    return lax.dot_general(a, b, dims, preferred_element_type=f32)


def swap(value, axis):
    return lax.ppermute(value, axis, [(0, 1), (1, 0)])


def shifts(size):
    return sorted(range(1, size), key=lambda k: -min(k, size - k) == -size // 2)


def scatter_sum(value, axis, size):
    me = lax.axis_index(axis)
    rows = value.shape[0] // size
    total = lax.dynamic_slice_in_dim(value, me * rows, rows, 0)
    parts = []
    for k in range(1, size):
        block = lax.dynamic_slice_in_dim(value, (me + k) % size * rows, rows, 0)
        parts.append(lax.ppermute(block, axis, [(j, (j + k) % size) for j in range(size)]))
    for part in parts:
        total = total + part
    return total


def gather_rows(value, axis, size):
    me = lax.axis_index(axis)
    rows = value.shape[0]
    parts = [value] + [
        lax.ppermute(value, axis, [(j, (j + k) % size) for j in range(size)])
        for k in range(1, size)
    ]
    whole = jnp.zeros((rows * size,) + value.shape[1:], value.dtype)
    for k, part in enumerate(parts):
        whole = lax.dynamic_update_slice_in_dim(whole, part, (me - k + size) % size * rows, 0)
    return whole


def replica_sum(term, sizes):
    total = scatter_sum(term, "core", sizes["core"])
    total = scatter_sum(total, "x", sizes["x"])
    total = scatter_sum(total, "y", sizes["y"])
    total = total + swap(total, "zh")
    total = gather_rows(total, "y", sizes["y"])
    total = gather_rows(total, "x", sizes["x"])
    return gather_rows(total, "core", sizes["core"])


def body(sizes, activations, norm_gain, key_weight, key_cotangent, outer_params, outer_momentum, fragment):
    n = sizes["fsdp"]
    tokens, model_width = activations.shape
    key_width = key_cotangent.shape[1]
    head_size = outer_params.shape[1]
    shard = key_weight.shape[1]
    rows = shard // PIECES
    factor = model_width ** (-0.5)
    me = lax.axis_index("fsdp")
    weight = key_weight[0]
    gain = norm_gain[0].astype(f32)[:, None]

    scaled = (weight.astype(f32) * gain).astype(bf16)
    to_right = [scaled[c * rows : (c + 1) * rows] for c in range(PIECES)]
    to_left = to_right
    got_right, got_left = [], []
    for c in range(PIECES):
        got_right.append(lax.ppermute(to_right[c], "fsdp", RIGHT))
        got_left.append(lax.ppermute(to_left[c], "fsdp", LEFT))

    xfloat = activations.astype(f32)
    inverse = lax.rsqrt(jnp.mean(xfloat * xfloat, axis=1, keepdims=True) + epsilon)
    cotangent = (key_cotangent.astype(f32) * inverse).astype(bf16)

    def own_partial(owner, c):
        start = jnp.clip(owner, 0, n - 1) * shard + c * rows
        columns = lax.dynamic_slice_in_dim(activations, start, rows, 1)
        return dot(columns, cotangent, CONTRACT_ROWS)

    arrived_right, arrived_left = [got_right], [got_left]
    for s in range(1, n):
        next_right, next_left = [], []
        for c in range(PIECES):
            part = jnp.where(me < s, own_partial(n - s + me, c), 0.0)
            out = (got_right[c].astype(f32) + part).astype(bf16)
            next_right.append(lax.ppermute(out, "fsdp", RIGHT))
            part = jnp.where(me > n - 1 - s, own_partial(me + s - n, c), 0.0)
            out = (got_left[c].astype(f32) + part).astype(bf16)
            next_left.append(lax.ppermute(out, "fsdp", LEFT))
        got_right, got_left = next_right, next_left
        if s < n - 1:
            arrived_right.append(got_right)
            arrived_left.append(got_left)

    whole = jnp.zeros((model_width, key_width), bf16)
    whole = lax.dynamic_update_slice_in_dim(whole, scaled, me * shard, 0)
    for o in range(1, n):
        for c in range(PIECES):
            piece = jnp.where(me >= o, arrived_right[o - 1][c], arrived_left[n - 1 - o][c])
            whole = lax.dynamic_update_slice_in_dim(whole, piece, (me - o + n) % n * shard + c * rows, 0)

    keys_float = dot(activations, whole) * (inverse * factor)
    keys = keys_float.astype(bf16)
    project = jnp.sum(keys_float * key_cotangent.astype(f32), axis=1, keepdims=True) / model_width
    adjusted = dot(key_cotangent, whole, CONTRACT_COLUMNS) * factor
    input_grad = (inverse * (adjusted - xfloat * (inverse * project))).astype(bf16)

    weight_grad, gain_grad = [], []
    for c in range(PIECES):
        summed = (got_right[c].astype(f32) + got_left[c].astype(f32) + own_partial(me, c)) * factor
        part = slice(c * rows, (c + 1) * rows)
        weight_grad.append((summed * gain[part]).astype(bf16))
        gain_grad.append(jnp.sum(summed * weight[part].astype(f32), axis=1))
    weight_grad = jnp.concatenate(weight_grad, 0)[None]
    gain_grad = jnp.concatenate(gain_grad, 0)[None]

    column_start = fragment[0] % (key_width // head_size) * head_size
    local_block = lax.dynamic_slice_in_dim(weight, column_start, head_size, 1).astype(f32)
    replicas = sizes["x"] * sizes["y"] * sizes["zh"] * sizes["core"]
    increment = replica_sum(outer_params - local_block, sizes) / replicas
    new_momentum = momentum_decay * outer_momentum + increment
    new_params = outer_params - outer_rate * (increment + momentum_decay * new_momentum)
    return (keys, input_grad, weight_grad, gain_grad, new_params, new_momentum)


def solution(mesh):
    sizes = {"x": 4, "y": 4, "zh": 2, "core": 2, "fsdp": 4}
    fine = Mesh(mesh.devices.reshape(tuple(sizes.values())), tuple(sizes))
    rep = ("x", "y", "zh", "core")
    both = rep + ("fsdp",)
    in_specs = (
        P(both, None),
        P(rep, "fsdp"),
        P(rep, "fsdp", None),
        P(both, None),
        P("fsdp", None),
        P("fsdp", None),
        P(),
    )
    out_specs = (
        P(both, None),
        P(both, None),
        P(rep, "fsdp", None),
        P(rep, "fsdp"),
        P("fsdp", None),
        P("fsdp", None),
    )

    def local(*args):
        return body(sizes, *args)

    return jax.shard_map(local, mesh=fine, in_specs=in_specs, out_specs=out_specs, check_vma=False)
```

```python
import functools

import jax
import jax.numpy as jnp
from jax import lax
from jax.experimental import pallas as pl
from jax.experimental.pallas import tpu as pltpu
from jax.sharding import Mesh, PartitionSpec as P

outer_rate = 0.7
momentum_decay = 0.9
epsilon = 1e-05

PIECES = 2
CONTRACT_ROWS = (((0,), (0,)), ((), ()))
CONTRACT_COLUMNS = (((1,), (1,)), ((), ()))
PLAIN = (((1,), (0,)), ((), ()))
f32, bf16 = jnp.float32, jnp.bfloat16


def dot(a, b, dims=PLAIN):
    return lax.dot_general(a, b, dims, preferred_element_type=f32)


def place(me, mirrored, n):
    return jnp.where(mirrored == 1, n - 1 - me, me)


def pass_on_kernel(n, s, c, inputs, split, me_ref, x_ref, c_ref, *refs):
    there, back = refs[0], refs[1]
    outs = refs[inputs:]
    columns, held, sems = refs[-3:]
    me, mirrored = me_ref[0], me_ref[1]
    rows, block = held.shape[1], columns.shape[3]
    steps = rows // block
    part = rows // split
    ways = ((there, n - s + me, me < s), (back, me + s - n, me > n - 1 - s))

    def some(j):
        return pl.ds(j * block, block)

    def columns_in(d, j):
        first = place(ways[d][1], mirrored, n) * (rows * PIECES) + c * rows + j * block
        source = x_ref.at[:, pl.ds(pl.multiple_of(first, block), block)]
        return pltpu.make_async_copy(source, columns.at[d, j], sems.at[d, j, 0])

    def sum_in(d, j):
        return pltpu.make_async_copy(ways[d][0].at[some(j)], held.at[d, some(j)], sems.at[d, j, 1])

    def sum_out(d, j):
        target = outs[d * split + j * block // part].at[pl.ds(j * block % part, block)]
        return pltpu.make_async_copy(held.at[d, some(j)], target, sems.at[d, j, 2])

    def fetch(d):
        for j in range(steps):
            columns_in(d, j).start()
            sum_in(d, j).start()

    def add(d):
        for j in range(steps):
            columns_in(d, j).wait()
            sum_in(d, j).wait()
            term = dot(columns[d, j], c_ref[...], CONTRACT_ROWS)
            held[d, some(j)] = (held[d, some(j)].astype(f32) + term).astype(bf16)
            sum_out(d, j).start()

    def finish(d):
        for j in range(steps):
            sum_out(d, j).wait()

    for step in (fetch, add, finish):
        for d in range(2):
            pl.when(ways[d][2])(functools.partial(step, d))


def pass_on(s, c, n, me, activations, cotangent, there, back, tokens=(), rider=None, split=1):
    rows, key_width = there.shape
    tokens_here = activations.shape[0]
    block = 256
    any_spec = pl.BlockSpec(memory_space=pl.ANY)
    riders = [] if rider is None else [rider]
    operands = [there, back, *riders, *tokens]
    last = s == n - 1
    outs = [jax.ShapeDtypeStruct((rows // split, key_width), bf16)] * (2 * split)
    outs += [jax.ShapeDtypeStruct(r.shape, r.dtype) for r in riders]
    aliases = {} if last else {3: 0, 4: 1}
    if riders:
        aliases[5] = len(outs) - 1
    return pl.pallas_call(
        functools.partial(pass_on_kernel, n, s, c, len(operands), split),
        out_shape=outs,
        in_specs=[
            pl.BlockSpec(memory_space=pltpu.SMEM),
            any_spec,
            pl.BlockSpec(memory_space=pltpu.VMEM),
        ]
        + [any_spec] * len(operands),
        out_specs=[any_spec] * len(outs),
        scratch_shapes=[
            pltpu.VMEM((2, rows // block, tokens_here, block), bf16),
            pltpu.VMEM((2, rows, key_width), bf16),
            pltpu.SemaphoreType.DMA((2, rows // block, 3)),
        ],
        input_output_aliases=aliases,
        compiler_params=pltpu.CompilerParams(vmem_limit_bytes=56 * 2**20),
        cost_estimate=pl.CostEstimate(
            flops=10**11 if (s, c) == (2, 0) else 0, bytes_accessed=4 * 2**20, transcendentals=0
        ),
    )(me, activations, cotangent, *operands)


def project_kernel(n, factor, tokens, me_ref, x_ref, c_ref, inverse_ref, *refs):
    own, from_left, from_right = refs[:PIECES], [], []
    at = PIECES
    for _ in range(n - 1):
        from_left.append(refs[at : at + PIECES])
        at += PIECES
    for _ in range(n - 1):
        from_right.append(refs[at : at + PIECES])
        at += PIECES
    keys_ref, grad_ref, held, total, adjusted, sems = refs[at + tokens :]
    me, mirrored = me_ref[0], me_ref[1]
    rows = held.shape[1]
    model_width = x_ref.shape[1]
    order = [(o, c) for o in (0, 2, 1, 3) for c in range(PIECES)]

    def fetch(index):
        o, c = order[index]
        slot = index % 4

        def start(ref):
            pltpu.make_async_copy(ref, held.at[slot], sems.at[slot]).start()

        if o == 0:
            start(own[c])
        else:
            pl.when(me >= o)(lambda: start(from_left[o - 1][c]))
            pl.when(me < o)(lambda: start(from_right[n - 1 - o][c]))

    for index in range(3):
        fetch(index)
    cotangent = c_ref[...]
    for index, (o, c) in enumerate(order):
        if index + 3 < len(order):
            fetch(index + 3)
        slot = index % 4
        pltpu.make_async_copy(own[0], held.at[slot], sems.at[slot]).wait()
        owner = place(lax.rem(me - o + n, n), mirrored, n)
        start = pl.multiple_of(owner * (rows * PIECES) + c * rows, 128)
        columns = pl.ds(start, rows)
        part = dot(x_ref[:, columns], held[slot])
        if index == 0:
            total[...] = part
        else:
            total[...] += part
        adjusted[:, columns] = dot(cotangent, held[slot], CONTRACT_COLUMNS)
    inverse = inverse_ref[...]
    keys = total[...] * (inverse * factor)
    keys_ref[...] = keys.astype(bf16)
    mean = jnp.sum(keys * cotangent.astype(f32), axis=1, keepdims=True) * (1.0 / model_width)
    scale = inverse * factor
    take = inverse * inverse * mean
    for start in range(0, model_width, 1024):
        columns = slice(start, start + 1024)
        grad_ref[:, columns] = (
            scale * adjusted[:, columns] - x_ref[:, columns].astype(f32) * take
        ).astype(bf16)


def project(me, activations, key_cotangent, inverse, own, from_left, from_right, factor, waits):
    tokens, model_width = activations.shape
    key_width = key_cotangent.shape[1]
    n = len(from_left) + 1
    rows = own[0].shape[0]
    pieces = list(own)
    pieces += [p for ps in from_left for p in ps] + [p for ps in from_right for p in ps]
    pieces += waits
    vmem = pl.BlockSpec(memory_space=pltpu.VMEM)
    return pl.pallas_call(
        functools.partial(project_kernel, n, factor, len(waits)),
        out_shape=(
            jax.ShapeDtypeStruct((tokens, key_width), bf16),
            jax.ShapeDtypeStruct((tokens, model_width), bf16),
        ),
        in_specs=[pl.BlockSpec(memory_space=pltpu.SMEM), vmem, vmem, vmem]
        + [pl.BlockSpec(memory_space=pl.ANY)] * len(pieces),
        out_specs=(vmem, vmem),
        scratch_shapes=[
            pltpu.VMEM((4, rows, key_width), bf16),
            pltpu.VMEM((tokens, key_width), f32),
            pltpu.VMEM((tokens, model_width), f32),
            pltpu.SemaphoreType.DMA((4,)),
        ],
        compiler_params=pltpu.CompilerParams(vmem_limit_bytes=28 * 2**20),
        cost_estimate=pl.CostEstimate(
            flops=4 * tokens * model_width * key_width,
            bytes_accessed=16 * 2**20,
            transcendentals=0,
        ),
    )(me, activations, key_cotangent, inverse, *pieces)


def weight_kernel(factor, first, x_ref, c_ref, right_ref, left_ref, weight_ref, gain_ref, *refs):
    grad_ref, gain_grad_ref, grad, gain_grad, sems = refs[-5:]
    rows, width = grad.shape
    block = 256
    gain = jnp.broadcast_to(gain_ref[:, first : first + rows].astype(f32) * factor, (128, rows)).T
    copies = []
    for j in range(0, rows, block):
        some, mine = slice(j, j + block), slice(first + j, first + j + block)
        own = dot(x_ref[:, mine], c_ref[...], CONTRACT_ROWS)
        folded = None
        for start in range(0, width, 128):
            lanes = slice(start, start + 128)
            summed = own[:, lanes] + right_ref[some, lanes].astype(f32) + left_ref[some, lanes].astype(f32)
            grad[some, lanes] = (summed * gain[some]).astype(bf16)
            terms = summed * weight_ref[mine, lanes].astype(f32)
            folded = terms if folded is None else folded + terms
        copies.append(pltpu.make_async_copy(grad.at[some], grad_ref.at[mine], sems.at[j // block]))
        copies[-1].start()
        gain_grad[:, some] = jnp.sum(folded.T, axis=0, keepdims=True) * factor
    copies.append(
        pltpu.make_async_copy(
            gain_grad, gain_grad_ref.at[:, first : first + rows], sems.at[rows // block]
        )
    )
    copies[-1].start()
    for copy in copies:
        copy.wait()


def weight_piece(factor, first, columns, cotangent, right, left, weight, gain, so_far):
    shard, key_width = weight.shape
    rows = right.shape[0]
    any_spec = pl.BlockSpec(memory_space=pl.ANY)
    operands = [columns, cotangent, right, left, weight, gain]
    in_specs = [pl.BlockSpec(memory_space=pltpu.VMEM)] * len(operands)
    aliases = {}
    if so_far is not None:
        aliases = {len(operands): 0, len(operands) + 1: 1}
        in_specs += [any_spec, any_spec]
        operands += list(so_far)
    return pl.pallas_call(
        functools.partial(weight_kernel, factor, first),
        out_shape=(
            jax.ShapeDtypeStruct((shard, key_width), bf16),
            jax.ShapeDtypeStruct((1, shard), f32),
        ),
        in_specs=in_specs,
        out_specs=(any_spec, any_spec),
        scratch_shapes=[
            pltpu.VMEM((rows, key_width), bf16),
            pltpu.VMEM((1, rows), f32),
            pltpu.SemaphoreType.DMA((rows // 256 + 1,)),
        ],
        input_output_aliases=aliases,
        compiler_params=pltpu.CompilerParams(vmem_limit_bytes=16 * 2**20),
        cost_estimate=pl.CostEstimate(flops=0, bytes_accessed=4 * 2**20, transcendentals=0),
    )(*operands)


def body(sizes, activations, norm_gain, key_weight, key_cotangent, outer_params, outer_momentum, fragment):
    n = sizes["fsdp"]
    tokens, model_width = activations.shape
    key_width = key_cotangent.shape[1]
    head_size = outer_params.shape[1]
    shard = key_weight.shape[1]
    factor = model_width ** (-0.5)
    weight = key_weight[0]
    mirrored = lax.axis_index("core")
    me = place(lax.axis_index("fsdp"), mirrored, n)
    where_am_i = jnp.stack([me, mirrored]).astype(jnp.int32)
    line = ("core", "fsdp")
    up = [(j, j + 1) for j in range(n - 1)] + [(n + j + 1, n + j) for j in range(n - 1)]
    down = [(j, i) for i, j in up]

    def send(there, back):
        return [lax.ppermute(there, line, up), lax.ppermute(back, line, down)]

    gain = norm_gain[0].astype(f32)[:, None]
    rows = shard // PIECES

    def scaled(weight, c):
        part = slice(c * rows, (c + 1) * rows)
        return (weight[part].astype(f32) * gain[part]).astype(bf16)

    first = scaled(weight, 0)
    first, weight, activations = lax.optimization_barrier((first, weight, activations))
    own, flying = [first], [send(first, first)]

    column_start = fragment[0] % (key_width // head_size) * head_size
    local_block = lax.dynamic_slice_in_dim(weight, column_start, head_size, 1)
    plane = ("x", "y", "core")
    owners = sizes["x"] * sizes["y"] * sizes["core"]
    spread = (owners, shard // owners, head_size)
    delta = (outer_params - local_block.astype(f32)).reshape(spread)

    xfloat = activations.astype(f32)
    inverse = lax.rsqrt(jnp.mean(xfloat * xfloat, axis=1, keepdims=True) + epsilon)
    cotangent = (key_cotangent.astype(f32) * inverse).astype(bf16)
    weight, delta, cotangent = lax.optimization_barrier((weight, delta, cotangent))
    for c in range(1, PIECES):
        piece = scaled(weight, c)
        piece, delta = lax.optimization_barrier((piece, delta))
        own.append(piece)
        flying.append(send(piece, piece))
    delta = lax.all_to_all(delta, plane, 0, 0, tiled=True)

    from_near, from_far, last_parts = [], [], []
    before = ()
    for s in range(1, n):
        passed_there, passed_back, following = [], [], []
        for c in range(PIECES):
            there, back = flying[c]
            last = s == n - 1
            split = 1
            tokens, rider = list(before), None
            if (s, c) == (1, 1):
                total = jnp.sum(delta, axis=0)
            if (s, c) in ((1, 1), (2, 1)):
                rider = total
            if (s, c) == (2, 0):
                tokens.append(total)
            outs = pass_on(
                s, c, n, where_am_i, activations, cotangent, there, back, tokens, rider, split
            )
            if (s, c) == (1, 1):
                total = outs[-1] + lax.ppermute(outs[-1], "zh", [(0, 1), (1, 0)])
            if (s, c) == (2, 1):
                delta = jnp.broadcast_to(outs[-1][None], spread)
                delta = lax.all_to_all(delta, plane, 0, 0, tiled=True)
            before = outs[: 2 * split]
            passed_there.append(there if last else outs[0])
            passed_back.append(back if last else outs[1])
            following += [send(*pair) for pair in zip(outs[:split], outs[split : 2 * split])]
        flying = following
        from_near.append(passed_there)
        from_far.append(passed_back)

    keys, input_grad = project(
        where_am_i, activations, key_cotangent, inverse, own, from_near, from_far, factor, list(before)
    )
    keys, delta = lax.optimization_barrier((keys, delta))

    replicas = sizes["x"] * sizes["y"] * sizes["zh"] * sizes["core"]
    increment = delta.reshape(outer_params.shape) / replicas
    new_momentum = momentum_decay * outer_momentum + increment
    new_params = outer_params - outer_rate * (increment + momentum_decay * new_momentum)

    columns = lax.dynamic_slice_in_dim(activations, lax.axis_index("fsdp") * shard, shard, 1)
    so_far, start = None, 0
    for right, left in flying:
        so_far = weight_piece(
            factor, start, columns, cotangent, right, left, weight, norm_gain, so_far
        )
        start += right.shape[0]
    weight_grad, gain_grad = so_far
    return (keys, input_grad, weight_grad[None], gain_grad, new_params, new_momentum)


def solution(mesh):
    sizes = {"x": 4, "y": 4, "zh": 2, "core": 2, "fsdp": 4}
    fine = Mesh(mesh.devices.reshape(tuple(sizes.values())), tuple(sizes))
    rep = ("x", "y", "zh", "core")
    both = rep + ("fsdp",)
    in_specs = (
        P(both, None),
        P(rep, "fsdp"),
        P(rep, "fsdp", None),
        P(both, None),
        P("fsdp", None),
        P("fsdp", None),
        P(),
    )
    out_specs = (
        P(both, None),
        P(both, None),
        P(rep, "fsdp", None),
        P(rep, "fsdp"),
        P("fsdp", None),
        P("fsdp", None),
    )

    def local(*args):
        return body(sizes, *args)

    return jax.shard_map(local, mesh=fine, in_specs=in_specs, out_specs=out_specs, check_vma=False)
```

```python
import functools

import jax
import jax.numpy as jnp
from jax import lax
from jax.experimental import pallas as pl
from jax.experimental.pallas import tpu as pltpu
from jax.sharding import Mesh, PartitionSpec as P

outer_rate = 0.7
momentum_decay = 0.9
epsilon = 1e-05

PIECES = 2
CONTRACT_ROWS = (((0,), (0,)), ((), ()))
CONTRACT_COLUMNS = (((1,), (1,)), ((), ()))
PLAIN = (((1,), (0,)), ((), ()))
f32, bf16 = jnp.float32, jnp.bfloat16


def dot(a, b, dims=PLAIN):
    return lax.dot_general(a, b, dims, preferred_element_type=f32)


def place(me, mirrored, n):
    return jnp.where(mirrored == 1, n - 1 - me, me)


def scale_kernel(weight_ref, gain_ref, out_ref, gain_row, held, scaled, sems):
    rows, width = held.shape
    block = rows // sems.shape[0]

    def copy(j, k):
        some = pl.ds(j * block, block)
        source, target = ((weight_ref, held), (scaled, out_ref))[k]
        return pltpu.make_async_copy(source.at[some], target.at[some], sems.at[j, k])

    gain_in = pltpu.make_async_copy(gain_ref, gain_row, sems.at[0, 2])
    gain_in.start()
    for j in range(rows // block):
        copy(j, 0).start()
    gain_in.wait()
    gain = jnp.broadcast_to(gain_row[:, :rows].astype(f32), (128, rows)).T
    for j in range(rows // block):
        some = slice(j * block, (j + 1) * block)
        copy(j, 0).wait()
        for start in range(0, width, 128):
            lanes = slice(start, start + 128)
            scaled[some, lanes] = (held[some, lanes].astype(f32) * gain[some]).astype(bf16)
        copy(j, 1).start()
    for j in range(rows // block):
        copy(j, 1).wait()


def scale_first(weight, gain, rows):
    key_width = weight.shape[1]
    any_spec = pl.BlockSpec(memory_space=pl.ANY)
    return pl.pallas_call(
        scale_kernel,
        out_shape=jax.ShapeDtypeStruct((rows, key_width), bf16),
        in_specs=[any_spec, any_spec],
        out_specs=any_spec,
        scratch_shapes=[
            pltpu.VMEM(gain.shape, bf16),
            pltpu.VMEM((rows, key_width), bf16),
            pltpu.VMEM((rows, key_width), bf16),
            pltpu.SemaphoreType.DMA((4, 3)),
        ],
        compiler_params=pltpu.CompilerParams(vmem_limit_bytes=56 * 2**20),
        cost_estimate=pl.CostEstimate(flops=0, bytes_accessed=2 * 2**20, transcendentals=0),
    )(weight, gain)


def pass_on_kernel(n, s, c, inputs, split, me_ref, x_ref, c_ref, *refs):
    there, back = refs[0], refs[1]
    outs = refs[inputs:]
    cotangent, columns, held, sems = refs[-4:]
    me, mirrored = me_ref[0], me_ref[1]
    rows, block = held.shape[1], columns.shape[3]
    steps = rows // block
    part = rows // split
    ways = ((there, n - s + me, me < s), (back, me + s - n, me > n - 1 - s))

    def some(j):
        return pl.ds(j * block, block)

    def columns_in(d, j):
        first = place(ways[d][1], mirrored, n) * (rows * PIECES) + c * rows + j * block
        source = x_ref.at[:, pl.ds(pl.multiple_of(first, block), block)]
        return pltpu.make_async_copy(source, columns.at[d, j], sems.at[d, j, 0])

    def sum_in(d, j):
        return pltpu.make_async_copy(ways[d][0].at[some(j)], held.at[d, some(j)], sems.at[d, j, 1])

    def sum_out(d, j):
        target = outs[d * split + j * block // part].at[pl.ds(j * block % part, block)]
        return pltpu.make_async_copy(held.at[d, some(j)], target, sems.at[d, j, 2])

    def cotangent_in(d):
        return pltpu.make_async_copy(c_ref, cotangent.at[d], sems.at[d, 0, 3])

    def fetch(d):
        cotangent_in(d).start()
        for j in range(steps):
            columns_in(d, j).start()
            sum_in(d, j).start()

    def add(d):
        cotangent_in(d).wait()
        for j in range(steps):
            columns_in(d, j).wait()
            sum_in(d, j).wait()
            term = dot(columns[d, j], cotangent[d], CONTRACT_ROWS)
            held[d, some(j)] = (held[d, some(j)].astype(f32) + term).astype(bf16)
            sum_out(d, j).start()

    def finish(d):
        for j in range(steps):
            sum_out(d, j).wait()

    for step in (fetch, add, finish):
        for d in range(2):
            pl.when(ways[d][2])(functools.partial(step, d))


def pass_on(s, c, n, me, activations, cotangent, there, back, tokens=(), rider=None, split=1):
    rows, key_width = there.shape
    tokens_here = activations.shape[0]
    block = 256
    any_spec = pl.BlockSpec(memory_space=pl.ANY)
    riders = [] if rider is None else [rider]
    operands = [there, back, *riders, *tokens]
    last = s == n - 1
    outs = [jax.ShapeDtypeStruct((rows // split, key_width), bf16)] * (2 * split)
    outs += [jax.ShapeDtypeStruct(r.shape, r.dtype) for r in riders]
    aliases = {} if last else {3: 0, 4: 1}
    if riders:
        aliases[5] = len(outs) - 1
    return pl.pallas_call(
        functools.partial(pass_on_kernel, n, s, c, len(operands), split),
        out_shape=outs,
        in_specs=[
            pl.BlockSpec(memory_space=pltpu.SMEM),
            any_spec,
            any_spec,
        ]
        + [any_spec] * len(operands),
        out_specs=[any_spec] * len(outs),
        scratch_shapes=[
            pltpu.VMEM((2, tokens_here, key_width), bf16),
            pltpu.VMEM((2, rows // block, tokens_here, block), bf16),
            pltpu.VMEM((2, rows, key_width), bf16),
            pltpu.SemaphoreType.DMA((2, rows // block, 4)),
        ],
        input_output_aliases=aliases,
        compiler_params=pltpu.CompilerParams(vmem_limit_bytes=56 * 2**20),
        cost_estimate=pl.CostEstimate(
            flops=10**11 if (s, c) == (2, 0) else 0, bytes_accessed=4 * 2**20, transcendentals=0
        ),
    )(me, activations, cotangent, *operands)


def project_kernel(n, factor, tokens, me_ref, x_ref, c_ref, inverse_ref, *refs):
    own, from_left, from_right = refs[:PIECES], [], []
    at = PIECES
    for _ in range(n - 1):
        from_left.append(refs[at : at + PIECES])
        at += PIECES
    for _ in range(n - 1):
        from_right.append(refs[at : at + PIECES])
        at += PIECES
    keys_ref, grad_ref, held, total, adjusted, sems = refs[at + tokens :]
    me, mirrored = me_ref[0], me_ref[1]
    rows = held.shape[1]
    model_width = x_ref.shape[1]
    order = [(o, c) for o in (0, 2, 1, 3) for c in range(PIECES)]

    def fetch(index):
        o, c = order[index]
        slot = index % 4

        def start(ref):
            pltpu.make_async_copy(ref, held.at[slot], sems.at[slot]).start()

        if o == 0:
            start(own[c])
        else:
            pl.when(me >= o)(lambda: start(from_left[o - 1][c]))
            pl.when(me < o)(lambda: start(from_right[n - 1 - o][c]))

    for index in range(3):
        fetch(index)
    cotangent = c_ref[...]
    for index, (o, c) in enumerate(order):
        if index + 3 < len(order):
            fetch(index + 3)
        slot = index % 4
        pltpu.make_async_copy(own[0], held.at[slot], sems.at[slot]).wait()
        owner = place(lax.rem(me - o + n, n), mirrored, n)
        start = pl.multiple_of(owner * (rows * PIECES) + c * rows, 128)
        columns = pl.ds(start, rows)
        part = dot(x_ref[:, columns], held[slot])
        if index == 0:
            total[...] = part
        else:
            total[...] += part
        adjusted[:, columns] = dot(cotangent, held[slot], CONTRACT_COLUMNS)
    inverse = inverse_ref[...]
    keys = total[...] * (inverse * factor)
    keys_ref[...] = keys.astype(bf16)
    mean = jnp.sum(keys * cotangent.astype(f32), axis=1, keepdims=True) * (1.0 / model_width)
    scale = inverse * factor
    take = inverse * inverse * mean
    for start in range(0, model_width, 1024):
        columns = slice(start, start + 1024)
        grad_ref[:, columns] = (
            scale * adjusted[:, columns] - x_ref[:, columns].astype(f32) * take
        ).astype(bf16)


def project(me, activations, key_cotangent, inverse, own, from_left, from_right, factor, waits):
    tokens, model_width = activations.shape
    key_width = key_cotangent.shape[1]
    n = len(from_left) + 1
    rows = own[0].shape[0]
    pieces = list(own)
    pieces += [p for ps in from_left for p in ps] + [p for ps in from_right for p in ps]
    pieces += waits
    vmem = pl.BlockSpec(memory_space=pltpu.VMEM)
    return pl.pallas_call(
        functools.partial(project_kernel, n, factor, len(waits)),
        out_shape=(
            jax.ShapeDtypeStruct((tokens, key_width), bf16),
            jax.ShapeDtypeStruct((tokens, model_width), bf16),
        ),
        in_specs=[pl.BlockSpec(memory_space=pltpu.SMEM), vmem, vmem, vmem]
        + [pl.BlockSpec(memory_space=pl.ANY)] * len(pieces),
        out_specs=(vmem, vmem),
        scratch_shapes=[
            pltpu.VMEM((4, rows, key_width), bf16),
            pltpu.VMEM((tokens, key_width), f32),
            pltpu.VMEM((tokens, model_width), f32),
            pltpu.SemaphoreType.DMA((4,)),
        ],
        compiler_params=pltpu.CompilerParams(vmem_limit_bytes=28 * 2**20),
        cost_estimate=pl.CostEstimate(
            flops=4 * tokens * model_width * key_width,
            bytes_accessed=16 * 2**20,
            transcendentals=0,
        ),
    )(me, activations, key_cotangent, inverse, *pieces)


def weight_kernel(factor, first, own_ref, right_ref, left_ref, weight_ref, gain_ref, *refs):
    grad_ref, gain_grad_ref, right, left, grad, gain_grad, sems = refs[-7:]
    rows, width = grad.shape
    block = rows // (sems.shape[0] - 1)
    steps = rows // block

    def copy(j, k):
        some, mine = slice(j * block, (j + 1) * block), slice(first + j * block, first + (j + 1) * block)
        source = (right_ref, left_ref, grad)[k].at[some]
        target = grad_ref.at[mine] if k == 2 else (right, left)[k].at[some]
        return pltpu.make_async_copy(source, target, sems.at[j, k])

    for j in range(steps):
        copy(j, 0).start()
        copy(j, 1).start()
    gain = jnp.broadcast_to(gain_ref[:, first : first + rows].astype(f32) * factor, (128, rows)).T
    for j in range(steps):
        some, mine = slice(j * block, (j + 1) * block), slice(first + j * block, first + (j + 1) * block)
        copy(j, 0).wait()
        copy(j, 1).wait()
        folded = None
        for start in range(0, width, 128):
            lanes = slice(start, start + 128)
            summed = right[some, lanes].astype(f32) + left[some, lanes].astype(f32)
            summed = own_ref[some, lanes] + summed
            grad[some, lanes] = (summed * gain[some]).astype(bf16)
            terms = summed * weight_ref[mine, lanes].astype(f32)
            folded = terms if folded is None else folded + terms
        copy(j, 2).start()
        gain_grad[:, some] = jnp.sum(folded.T, axis=0, keepdims=True) * factor
    there = gain_grad_ref.at[:, first : first + rows]
    gain_out = pltpu.make_async_copy(gain_grad, there, sems.at[steps, 0])
    gain_out.start()
    for j in range(steps):
        copy(j, 2).wait()
    gain_out.wait()


def weight_piece(factor, first, own, right, left, weight, gain, so_far):
    shard, key_width = weight.shape
    rows = right.shape[0]
    any_spec = pl.BlockSpec(memory_space=pl.ANY)
    operands = [own, right, left, weight, gain]
    vmem = pl.BlockSpec(memory_space=pltpu.VMEM)
    in_specs = [vmem, any_spec, any_spec, vmem, vmem]
    aliases = {}
    if so_far is not None:
        aliases = {len(operands): 0, len(operands) + 1: 1}
        in_specs += [any_spec, any_spec]
        operands += list(so_far)
    return pl.pallas_call(
        functools.partial(weight_kernel, factor, first),
        out_shape=(
            jax.ShapeDtypeStruct((shard, key_width), bf16),
            jax.ShapeDtypeStruct((1, shard), f32),
        ),
        in_specs=in_specs,
        out_specs=(any_spec, any_spec),
        scratch_shapes=[
            pltpu.VMEM((rows, key_width), bf16),
            pltpu.VMEM((rows, key_width), bf16),
            pltpu.VMEM((rows, key_width), bf16),
            pltpu.VMEM((1, rows), f32),
            pltpu.SemaphoreType.DMA((rows // 256 + 1, 3)),
        ],
        input_output_aliases=aliases,
        compiler_params=pltpu.CompilerParams(vmem_limit_bytes=16 * 2**20),
        cost_estimate=pl.CostEstimate(flops=0, bytes_accessed=4 * 2**20, transcendentals=0),
    )(*operands)


def body(sizes, activations, norm_gain, key_weight, key_cotangent, outer_params, outer_momentum, fragment):
    n = sizes["fsdp"]
    tokens, model_width = activations.shape
    key_width = key_cotangent.shape[1]
    head_size = outer_params.shape[1]
    shard = key_weight.shape[1]
    factor = model_width ** (-0.5)
    weight = key_weight[0]
    mirrored = lax.axis_index("core")
    me = place(lax.axis_index("fsdp"), mirrored, n)
    where_am_i = jnp.stack([me, mirrored]).astype(jnp.int32)
    line = ("core", "fsdp")
    up = [(j, j + 1) for j in range(n - 1)] + [(n + j + 1, n + j) for j in range(n - 1)]
    down = [(j, i) for i, j in up]

    def send(there, back):
        return [lax.ppermute(there, line, up), lax.ppermute(back, line, down)]

    gain = norm_gain[0].astype(f32)[:, None]
    rows = shard // PIECES

    def scaled(weight, c):
        part = slice(c * rows, (c + 1) * rows)
        return (weight[part].astype(f32) * gain[part]).astype(bf16)

    first = scale_first(weight, norm_gain, rows)
    first, weight, activations = lax.optimization_barrier((first, weight, activations))
    own, flying = [first], [send(first, first)]

    column_start = fragment[0] % (key_width // head_size) * head_size
    local_block = lax.dynamic_slice_in_dim(weight, column_start, head_size, 1)
    plane = ("x", "y", "core")
    owners = sizes["x"] * sizes["y"] * sizes["core"]
    spread = (owners, shard // owners, head_size)
    delta = (outer_params - local_block.astype(f32)).reshape(spread)

    xfloat = activations.astype(f32)
    inverse = lax.rsqrt(jnp.mean(xfloat * xfloat, axis=1, keepdims=True) + epsilon)
    cotangent = (key_cotangent.astype(f32) * inverse).astype(bf16)
    weight, delta, cotangent = lax.optimization_barrier((weight, delta, cotangent))
    for c in range(1, PIECES):
        piece = scaled(weight, c)
        piece, delta = lax.optimization_barrier((piece, delta))
        own.append(piece)
        flying.append(send(piece, piece))
    delta = lax.all_to_all(delta, plane, 0, 0, tiled=True)

    from_near, from_far, last_parts = [], [], []
    before = ()
    for s in range(1, n):
        passed_there, passed_back, following = [], [], []
        for c in range(PIECES):
            there, back = flying[c]
            last = s == n - 1
            split = 1
            tokens, rider = list(before), None
            if (s, c) == (1, 1):
                total = jnp.sum(delta, axis=0)
            if (s, c) == (2, 1):
                total = total + swapped
            if (s, c) in ((1, 1), (2, 1)):
                rider = total
            if (s, c) == (2, 0):
                tokens.append(swapped)
            outs = pass_on(
                s, c, n, where_am_i, activations, cotangent, there, back, tokens, rider, split
            )
            if (s, c) == (1, 1):
                swapped = lax.ppermute(outs[-1], "zh", [(0, 1), (1, 0)])
                total = outs[-1]
            if (s, c) == (2, 1):
                delta = jnp.broadcast_to(outs[-1][None], spread)
                delta = lax.all_to_all(delta, plane, 0, 0, tiled=True)
            before = outs[: 2 * split]
            passed_there.append(there if last else outs[0])
            passed_back.append(back if last else outs[1])
            following += [send(*pair) for pair in zip(outs[:split], outs[split : 2 * split])]
        flying = following
        from_near.append(passed_there)
        from_far.append(passed_back)

    keys, input_grad = project(
        where_am_i, activations, key_cotangent, inverse, own, from_near, from_far, factor, list(before)
    )
    keys, delta = lax.optimization_barrier((keys, delta))

    replicas = sizes["x"] * sizes["y"] * sizes["zh"] * sizes["core"]
    increment = delta.reshape(outer_params.shape) / replicas
    new_momentum = momentum_decay * outer_momentum + increment
    new_params = outer_params - outer_rate * (increment + momentum_decay * new_momentum)

    so_far = None
    for c, (right, left) in enumerate(flying):
        start = lax.axis_index("fsdp") * shard + c * rows
        columns = lax.dynamic_slice_in_dim(activations, start, rows, 1)
        term = dot(columns, cotangent, CONTRACT_ROWS)
        so_far = weight_piece(factor, c * rows, term, right, left, weight, norm_gain, so_far)
    weight_grad, gain_grad = so_far
    return (keys, input_grad, weight_grad[None], gain_grad, new_params, new_momentum)


def solution(mesh):
    sizes = {"x": 4, "y": 4, "zh": 2, "core": 2, "fsdp": 4}
    fine = Mesh(mesh.devices.reshape(tuple(sizes.values())), tuple(sizes))
    rep = ("x", "y", "zh", "core")
    both = rep + ("fsdp",)
    in_specs = (
        P(both, None),
        P(rep, "fsdp"),
        P(rep, "fsdp", None),
        P(both, None),
        P("fsdp", None),
        P("fsdp", None),
        P(),
    )
    out_specs = (
        P(both, None),
        P(both, None),
        P(rep, "fsdp", None),
        P(rep, "fsdp"),
        P("fsdp", None),
        P("fsdp", None),
    )

    def local(*args):
        return body(sizes, *args)

    return jax.shard_map(local, mesh=fine, in_specs=in_specs, out_specs=out_specs, check_vma=False)
```

```python
import functools

import jax
import jax.numpy as jnp
from jax import lax
from jax.experimental import pallas as pl
from jax.experimental.pallas import tpu as pltpu
from jax.sharding import Mesh, PartitionSpec as P

outer_rate = 0.7
momentum_decay = 0.9
epsilon = 1e-05

PIECES = 2
CONTRACT_ROWS = (((0,), (0,)), ((), ()))
CONTRACT_COLUMNS = (((1,), (1,)), ((), ()))
PLAIN = (((1,), (0,)), ((), ()))
f32, bf16 = jnp.float32, jnp.bfloat16


def dot(a, b, dims=PLAIN):
    return lax.dot_general(a, b, dims, preferred_element_type=f32)


def place(me, mirrored, n):
    return jnp.where(mirrored == 1, n - 1 - me, me)


def scale_kernel(weight_ref, gain_ref, out_ref, gain_row, held, scaled, sems):
    rows, width = held.shape
    block = rows // sems.shape[0]

    def copy(j, k):
        some = pl.ds(j * block, block)
        source, target = ((weight_ref, held), (scaled, out_ref))[k]
        return pltpu.make_async_copy(source.at[some], target.at[some], sems.at[j, k])

    gain_in = pltpu.make_async_copy(gain_ref, gain_row, sems.at[0, 2])
    gain_in.start()
    for j in range(rows // block):
        copy(j, 0).start()
    gain_in.wait()
    gain = jnp.broadcast_to(gain_row[:, :rows].astype(f32), (128, rows)).T
    for j in range(rows // block):
        some = slice(j * block, (j + 1) * block)
        copy(j, 0).wait()
        for start in range(0, width, 128):
            lanes = slice(start, start + 128)
            scaled[some, lanes] = (held[some, lanes].astype(f32) * gain[some]).astype(bf16)
        copy(j, 1).start()
    for j in range(rows // block):
        copy(j, 1).wait()


def scale_first(weight, gain, rows):
    key_width = weight.shape[1]
    any_spec = pl.BlockSpec(memory_space=pl.ANY)
    return pl.pallas_call(
        scale_kernel,
        out_shape=jax.ShapeDtypeStruct((rows, key_width), bf16),
        in_specs=[any_spec, any_spec],
        out_specs=any_spec,
        scratch_shapes=[
            pltpu.VMEM(gain.shape, bf16),
            pltpu.VMEM((rows, key_width), bf16),
            pltpu.VMEM((rows, key_width), bf16),
            pltpu.SemaphoreType.DMA((4, 3)),
        ],
        compiler_params=pltpu.CompilerParams(vmem_limit_bytes=56 * 2**20),
        cost_estimate=pl.CostEstimate(flops=0, bytes_accessed=2 * 2**20, transcendentals=0),
    )(weight, gain)


def pass_on_kernel(n, s, c, inputs, split, me_ref, x_ref, c_ref, *refs):
    there, back = refs[0], refs[1]
    outs = refs[inputs:]
    cotangent, columns, held, sems = refs[-4:]
    me, mirrored = me_ref[0], me_ref[1]
    rows, block = held.shape[1], columns.shape[3]
    steps = rows // block
    part = rows // split
    ways = ((there, n - s + me, me < s), (back, me + s - n, me > n - 1 - s))

    def some(j):
        return pl.ds(j * block, block)

    def columns_in(d, j):
        first = place(ways[d][1], mirrored, n) * (rows * PIECES) + c * rows + j * block
        source = x_ref.at[:, pl.ds(pl.multiple_of(first, block), block)]
        return pltpu.make_async_copy(source, columns.at[d, j], sems.at[d, j, 0])

    def sum_in(d, j):
        return pltpu.make_async_copy(ways[d][0].at[some(j)], held.at[d, some(j)], sems.at[d, j, 1])

    def sum_out(d, j):
        target = outs[d * split + j * block // part].at[pl.ds(j * block % part, block)]
        return pltpu.make_async_copy(held.at[d, some(j)], target, sems.at[d, j, 2])

    def cotangent_in(d):
        return pltpu.make_async_copy(c_ref, cotangent.at[d], sems.at[d, 0, 3])

    def fetch(d):
        cotangent_in(d).start()
        for j in range(steps):
            columns_in(d, j).start()
            sum_in(d, j).start()

    def add(d):
        cotangent_in(d).wait()
        for j in range(steps):
            columns_in(d, j).wait()
            sum_in(d, j).wait()
            term = dot(columns[d, j], cotangent[d], CONTRACT_ROWS)
            held[d, some(j)] = (held[d, some(j)].astype(f32) + term).astype(bf16)
            sum_out(d, j).start()

    def finish(d):
        for j in range(steps):
            sum_out(d, j).wait()

    for step in (fetch, add, finish):
        for d in range(2):
            pl.when(ways[d][2])(functools.partial(step, d))


def pass_on(s, c, n, me, activations, cotangent, there, back, tokens=(), rider=None, split=1):
    rows, key_width = there.shape
    tokens_here = activations.shape[0]
    block = 256
    any_spec = pl.BlockSpec(memory_space=pl.ANY)
    riders = [] if rider is None else [rider]
    operands = [there, back, *riders, *tokens]
    last = s == n - 1
    outs = [jax.ShapeDtypeStruct((rows // split, key_width), bf16)] * (2 * split)
    outs += [jax.ShapeDtypeStruct(r.shape, r.dtype) for r in riders]
    aliases = {} if last else {3: 0, 4: 1}
    if riders:
        aliases[5] = len(outs) - 1
    return pl.pallas_call(
        functools.partial(pass_on_kernel, n, s, c, len(operands), split),
        out_shape=outs,
        in_specs=[
            pl.BlockSpec(memory_space=pltpu.SMEM),
            any_spec,
            any_spec,
        ]
        + [any_spec] * len(operands),
        out_specs=[any_spec] * len(outs),
        scratch_shapes=[
            pltpu.VMEM((2, tokens_here, key_width), bf16),
            pltpu.VMEM((2, rows // block, tokens_here, block), bf16),
            pltpu.VMEM((2, rows, key_width), bf16),
            pltpu.SemaphoreType.DMA((2, rows // block, 4)),
        ],
        input_output_aliases=aliases,
        compiler_params=pltpu.CompilerParams(vmem_limit_bytes=56 * 2**20),
        cost_estimate=pl.CostEstimate(
            flops=10**11 if (s, c) == (2, 0) else 0, bytes_accessed=4 * 2**20, transcendentals=0
        ),
    )(me, activations, cotangent, *operands)


def project_kernel(n, factor, tokens, me_ref, x_ref, c_ref, inverse_ref, *refs):
    own, from_left, from_right = refs[:PIECES], [], []
    at = PIECES
    for _ in range(n - 1):
        from_left.append(refs[at : at + PIECES])
        at += PIECES
    for _ in range(n - 1):
        from_right.append(refs[at : at + PIECES])
        at += PIECES
    keys_ref, grad_ref, held, total, adjusted, sems = refs[at + tokens :]
    me, mirrored = me_ref[0], me_ref[1]
    rows = held.shape[1]
    model_width = x_ref.shape[1]
    order = [(o, c) for o in (0, 2, 1, 3) for c in range(PIECES)]

    def fetch(index):
        o, c = order[index]
        slot = index % 4

        def start(ref):
            pltpu.make_async_copy(ref, held.at[slot], sems.at[slot]).start()

        if o == 0:
            start(own[c])
        else:
            pl.when(me >= o)(lambda: start(from_left[o - 1][c]))
            pl.when(me < o)(lambda: start(from_right[n - 1 - o][c]))

    for index in range(3):
        fetch(index)
    cotangent = c_ref[...]
    for index, (o, c) in enumerate(order):
        if index + 3 < len(order):
            fetch(index + 3)
        slot = index % 4
        pltpu.make_async_copy(own[0], held.at[slot], sems.at[slot]).wait()
        owner = place(lax.rem(me - o + n, n), mirrored, n)
        start = pl.multiple_of(owner * (rows * PIECES) + c * rows, 128)
        columns = pl.ds(start, rows)
        part = dot(x_ref[:, columns], held[slot])
        if index == 0:
            total[...] = part
        else:
            total[...] += part
        adjusted[:, columns] = dot(cotangent, held[slot], CONTRACT_COLUMNS)
    inverse = inverse_ref[...]
    keys = total[...] * (inverse * factor)
    keys_ref[...] = keys.astype(bf16)
    mean = jnp.sum(keys * cotangent.astype(f32), axis=1, keepdims=True) * (1.0 / model_width)
    scale = inverse * factor
    take = inverse * inverse * mean
    for start in range(0, model_width, 1024):
        columns = slice(start, start + 1024)
        grad_ref[:, columns] = (
            scale * adjusted[:, columns] - x_ref[:, columns].astype(f32) * take
        ).astype(bf16)


def project(me, activations, key_cotangent, inverse, own, from_left, from_right, factor, waits):
    tokens, model_width = activations.shape
    key_width = key_cotangent.shape[1]
    n = len(from_left) + 1
    rows = own[0].shape[0]
    pieces = list(own)
    pieces += [p for ps in from_left for p in ps] + [p for ps in from_right for p in ps]
    pieces += waits
    vmem = pl.BlockSpec(memory_space=pltpu.VMEM)
    return pl.pallas_call(
        functools.partial(project_kernel, n, factor, len(waits)),
        out_shape=(
            jax.ShapeDtypeStruct((tokens, key_width), bf16),
            jax.ShapeDtypeStruct((tokens, model_width), bf16),
        ),
        in_specs=[pl.BlockSpec(memory_space=pltpu.SMEM), vmem, vmem, vmem]
        + [pl.BlockSpec(memory_space=pl.ANY)] * len(pieces),
        out_specs=(vmem, vmem),
        scratch_shapes=[
            pltpu.VMEM((4, rows, key_width), bf16),
            pltpu.VMEM((tokens, key_width), f32),
            pltpu.VMEM((tokens, model_width), f32),
            pltpu.SemaphoreType.DMA((4,)),
        ],
        compiler_params=pltpu.CompilerParams(vmem_limit_bytes=56 * 2**20),
        cost_estimate=pl.CostEstimate(
            flops=4 * tokens * model_width * key_width,
            bytes_accessed=16 * 2**20,
            transcendentals=0,
        ),
    )(me, activations, key_cotangent, inverse, *pieces)


def weight_kernel(factor, first, own_ref, right_ref, left_ref, weight_ref, gain_ref, *refs):
    grad_ref, gain_grad_ref, right, left, grad, gain_grad, sems = refs[-7:]
    rows, width = grad.shape
    block = rows // (sems.shape[0] - 1)
    steps = rows // block

    def copy(j, k):
        some, mine = slice(j * block, (j + 1) * block), slice(first + j * block, first + (j + 1) * block)
        source = (right_ref, left_ref, grad)[k].at[some]
        target = grad_ref.at[mine] if k == 2 else (right, left)[k].at[some]
        return pltpu.make_async_copy(source, target, sems.at[j, k])

    for j in range(steps):
        copy(j, 0).start()
        copy(j, 1).start()
    gain = jnp.broadcast_to(gain_ref[:, first : first + rows].astype(f32) * factor, (128, rows)).T
    for j in range(steps):
        some, mine = slice(j * block, (j + 1) * block), slice(first + j * block, first + (j + 1) * block)
        copy(j, 0).wait()
        copy(j, 1).wait()
        folded = None
        for start in range(0, width, 128):
            lanes = slice(start, start + 128)
            summed = right[some, lanes].astype(f32) + left[some, lanes].astype(f32)
            summed = own_ref[some, lanes] + summed
            grad[some, lanes] = (summed * gain[some]).astype(bf16)
            terms = summed * weight_ref[mine, lanes].astype(f32)
            folded = terms if folded is None else folded + terms
        copy(j, 2).start()
        gain_grad[:, some] = jnp.sum(folded.T, axis=0, keepdims=True) * factor
    there = gain_grad_ref.at[:, first : first + rows]
    gain_out = pltpu.make_async_copy(gain_grad, there, sems.at[steps, 0])
    gain_out.start()
    for j in range(steps):
        copy(j, 2).wait()
    gain_out.wait()


def weight_piece(factor, first, own, right, left, weight, gain, so_far):
    shard, key_width = weight.shape
    rows = right.shape[0]
    any_spec = pl.BlockSpec(memory_space=pl.ANY)
    operands = [own, right, left, weight, gain]
    vmem = pl.BlockSpec(memory_space=pltpu.VMEM)
    in_specs = [vmem, any_spec, any_spec, vmem, vmem]
    aliases = {}
    if so_far is not None:
        aliases = {len(operands): 0, len(operands) + 1: 1}
        in_specs += [any_spec, any_spec]
        operands += list(so_far)
    return pl.pallas_call(
        functools.partial(weight_kernel, factor, first),
        out_shape=(
            jax.ShapeDtypeStruct((shard, key_width), bf16),
            jax.ShapeDtypeStruct((1, shard), f32),
        ),
        in_specs=in_specs,
        out_specs=(any_spec, any_spec),
        scratch_shapes=[
            pltpu.VMEM((rows, key_width), bf16),
            pltpu.VMEM((rows, key_width), bf16),
            pltpu.VMEM((rows, key_width), bf16),
            pltpu.VMEM((1, rows), f32),
            pltpu.SemaphoreType.DMA((rows // 256 + 1, 3)),
        ],
        input_output_aliases=aliases,
        compiler_params=pltpu.CompilerParams(vmem_limit_bytes=16 * 2**20),
        cost_estimate=pl.CostEstimate(flops=0, bytes_accessed=4 * 2**20, transcendentals=0),
    )(*operands)


def body(sizes, activations, norm_gain, key_weight, key_cotangent, outer_params, outer_momentum, fragment):
    n = sizes["fsdp"]
    tokens, model_width = activations.shape
    key_width = key_cotangent.shape[1]
    head_size = outer_params.shape[1]
    shard = key_weight.shape[1]
    factor = model_width ** (-0.5)
    weight = key_weight[0]
    mirrored = lax.axis_index("core")
    me = place(lax.axis_index("fsdp"), mirrored, n)
    where_am_i = jnp.stack([me, mirrored]).astype(jnp.int32)
    line = ("core", "fsdp")
    up = [(j, j + 1) for j in range(n - 1)] + [(n + j + 1, n + j) for j in range(n - 1)]
    down = [(j, i) for i, j in up]

    def send(there, back):
        return [lax.ppermute(there, line, up), lax.ppermute(back, line, down)]

    gain = norm_gain[0].astype(f32)[:, None]
    rows = shard // PIECES

    def scaled(weight, c):
        part = slice(c * rows, (c + 1) * rows)
        return (weight[part].astype(f32) * gain[part]).astype(bf16)

    first = scale_first(weight, norm_gain, rows)
    first, weight, activations = lax.optimization_barrier((first, weight, activations))
    own, flying = [first], [send(first, first)]
    for c in range(1, PIECES):
        piece = scaled(weight, c)
        piece, weight, activations = lax.optimization_barrier((piece, weight, activations))
        own.append(piece)
        flying.append(send(piece, piece))

    column_start = fragment[0] % (key_width // head_size) * head_size
    local_block = lax.dynamic_slice_in_dim(weight, column_start, head_size, 1)
    plane = ("x", "y", "core")
    owners = sizes["x"] * sizes["y"] * sizes["core"]
    spread = (owners, shard // owners, head_size)
    delta = (outer_params - local_block.astype(f32)).reshape(spread)

    xfloat = activations.astype(f32)
    inverse = lax.rsqrt(jnp.mean(xfloat * xfloat, axis=1, keepdims=True) + epsilon)
    cotangent = (key_cotangent.astype(f32) * inverse).astype(bf16)
    delta = lax.all_to_all(delta, plane, 0, 0, tiled=True)

    from_near, from_far, last_parts = [], [], []
    before = ()
    for s in range(1, n):
        passed_there, passed_back, following = [], [], []
        for c in range(PIECES):
            there, back = flying[c]
            last = s == n - 1
            split = 1
            tokens, rider = list(before), None
            if (s, c) == (1, 1):
                total = jnp.sum(delta, axis=0)
            if (s, c) in ((1, 1), (2, 0), (2, 1)):
                rider = total
            if (s, c) == (2, 0):
                tokens.append(swapped)
            outs = pass_on(
                s, c, n, where_am_i, activations, cotangent, there, back, tokens, rider, split
            )
            if (s, c) == (1, 1):
                swapped = lax.ppermute(outs[-1], "zh", [(0, 1), (1, 0)])
                total = outs[-1]
            if (s, c) == (2, 0):
                total = outs[-1] + swapped
            if (s, c) == (2, 1):
                delta = jnp.broadcast_to(outs[-1][None], spread)
                delta = lax.all_to_all(delta, plane, 0, 0, tiled=True)
            before = outs[: 2 * split]
            passed_there.append(there if last else outs[0])
            passed_back.append(back if last else outs[1])
            following += [send(*pair) for pair in zip(outs[:split], outs[split : 2 * split])]
        flying = following
        from_near.append(passed_there)
        from_far.append(passed_back)

    keys, input_grad = project(
        where_am_i, activations, key_cotangent, inverse, own, from_near, from_far, factor, list(before)
    )
    keys, delta = lax.optimization_barrier((keys, delta))

    replicas = sizes["x"] * sizes["y"] * sizes["zh"] * sizes["core"]
    increment = delta.reshape(outer_params.shape) / replicas
    new_momentum = momentum_decay * outer_momentum + increment
    new_params = outer_params - outer_rate * (increment + momentum_decay * new_momentum)

    so_far = None
    for c, (right, left) in enumerate(flying):
        start = lax.axis_index("fsdp") * shard + c * rows
        columns = lax.dynamic_slice_in_dim(activations, start, rows, 1)
        term = dot(columns, cotangent, CONTRACT_ROWS)
        so_far = weight_piece(factor, c * rows, term, right, left, weight, norm_gain, so_far)
    weight_grad, gain_grad = so_far
    return (keys, input_grad, weight_grad[None], gain_grad, new_params, new_momentum)


def solution(mesh):
    sizes = {"x": 4, "y": 4, "zh": 2, "core": 2, "fsdp": 4}
    fine = Mesh(mesh.devices.reshape(tuple(sizes.values())), tuple(sizes))
    rep = ("x", "y", "zh", "core")
    both = rep + ("fsdp",)
    in_specs = (
        P(both, None),
        P(rep, "fsdp"),
        P(rep, "fsdp", None),
        P(both, None),
        P("fsdp", None),
        P("fsdp", None),
        P(),
    )
    out_specs = (
        P(both, None),
        P(both, None),
        P(rep, "fsdp", None),
        P(rep, "fsdp"),
        P("fsdp", None),
        P("fsdp", None),
    )

    def local(*args):
        return body(sizes, *args)

    return jax.shard_map(local, mesh=fine, in_specs=in_specs, out_specs=out_specs, check_vma=False)
```
